32 devices in a mesh: parts: 2 (over x), tp: 8 (over z, y), dp: 2 (over core).
Axes of the slice: x: 2, y: 2, z: 4, core: 2. Of those that a mesh axis runs over, the one named last changes fastest.
Arguments:
- tokens: bfloat16 [4, 512, 12288], P(('parts', 'dp'), None, 'tp'), parts along dimension 0, may hold values from -6 to 6
- cotangent: bfloat16 [4, 512, 12288], P(('parts', 'dp'), None, 'tp'), parts along dimension 0, may hold values from -6 to 6
- token_record_index: int32 [4, 512], P(('parts', 'dp')), parts along dimension 0, may hold values from 0 to 3, never falling along the last dimension, each value on 1 to 256 neighbouring positions
- query_weight: bfloat16 [12288, 12288], P('tp'), may hold values from -0.0546875 to 0.0546875
- adapter_down_weight: bfloat16 [12288, 16], P('tp'), may hold values from -0.0546875 to 0.0546875
- adapter_up_weight: bfloat16 [16, 12288], P(None, 'tp'), may hold values from -0.0546875 to 0.0546875
Outputs:
- query: bfloat16 [4, 512, 12288], P(('parts', 'dp'), None, 'tp'), parts along dimension 0
- adapter_a_grad: float32 [32, 12288], P('parts', 'tp'), parts along dimension 0
- adapter_b_grad: float32 [32, 12288], P('parts', 'tp'), parts along dimension 0
The draws below stay inside these ranges and needn't reach their ends.
There are 2 independent parts, one for each index of `parts`. The reference program is written for one: setup_inputs(seed, part) draws one part's arguments, and reference() takes and returns one part's arrays. A program takes and returns all parts, laid end to end along the dimension named above; an argument that names none is the same for every part. Nothing has to cross between parts.
Inputs may be any that keep to these rules, and one draw needn't show every extreme that they name: `token_record_index`: within each pack record numbers never fall, every record 0 to 3 has 1 to 256 tokens, and one record of each pack has exactly 256.
All inputs are finite; a program needn't handle non-finite values.
Results may differ from the reference program's by a relative error of at most 0.0034.
Values may be sent and summed in bfloat16 or wider, within the bound.
A program may use at most 256 MiB of HBM per device.

```python
import math
import jax
import jax.numpy as jnp
import numpy as np
from jax import lax

MODEL_WIDTH = 12288
ADAPTER_RANK = 16
PACK_RECORDS = 4
PACK_TOKENS = 512
N_DP = 2


def block_scale(own_key, dims, split, smallest, high):
    def one(axis_at, blocks):
        draws = jax.random.uniform(jax.random.fold_in(jax.random.fold_in(own_key, 6), axis_at), (blocks,), jnp.float32, smallest / len(split), high / len(split))
        return jnp.repeat(jnp.exp(draws), dims[axis_at] // blocks).reshape((-1,) + (1,) * (len(dims) - axis_at - 1))

    level = one(*split[0])
    for cut in split[1:]:
        level = level * one(*cut)
    return level


def length_profile(count, total, reach, lean):
    loads = [(1 << 20) // math.isqrt(grade ** lean) + 1 for grade in range(2, count + 1)]
    surplus, counts = total - reach - (count - 1), [1] * (count - 1)
    while surplus > 0:
        candidates = [i for i in range(count - 1) if counts[i] < reach]
        mass, left = sum([loads[i] for i in candidates]), surplus
        for i in candidates:
            more = min(reach - counts[i], max(1, left * loads[i] // mass), surplus)
            counts[i] = counts[i] + more
            surplus = surplus - more
    return np.array([reach] + counts)


def ragged_sizes(key, count, total, limit, slope):
    if count == 2:
        one = jax.random.randint(key, (), max(1, total - limit), min(limit, total - 1) + 1)
        return jnp.stack([one, total - one])
    sizes = jnp.asarray(length_profile(count, total, limit, slope), jnp.int32)
    twos = (count - 1) // 2
    giver, receiver = sizes[1:1 + 2 * twos:2], sizes[2:2 + 2 * twos:2]
    room = jnp.minimum(giver - 1, limit - receiver)
    shifted = jax.random.randint(jax.random.fold_in(key, 1), (twos,), 0, 1 << 20) % (room + 1)
    sizes = sizes.at[1:1 + 2 * twos:2].set(giver - shifted).at[2:2 + 2 * twos:2].set(receiver + shifted)
    return sizes[jax.random.permutation(jax.random.fold_in(key, 2), count)]


def centred(stream_key, dims, width, most, shards=(), held_as=jnp.bfloat16):
    loudness = block_scale(stream_key, dims, shards, -0.22, 0.18) if shards else 1.0
    entries = jax.random.normal(stream_key, dims, jnp.float32) * width * loudness
    return jnp.minimum(jnp.maximum(entries, -most), most).astype(held_as)


def setup_inputs(seed: int = 0, part: int = 0) -> dict:
    splits = jax.random.split(jax.random.key(seed), 7)
    part_splits = jax.random.split(jax.random.fold_in(splits[6], part), 7)
    return {
        "tokens": centred(part_splits[0], (N_DP, PACK_TOKENS, MODEL_WIDTH), 1.0, 6.0, ((0, 2), (2, 8))),
        "cotangent": centred(part_splits[1], (N_DP, PACK_TOKENS, MODEL_WIDTH), 1.0, 6.0, ((0, 2), (2, 8))),
        "token_record_index": jax.vmap(lambda own: jnp.searchsorted(jnp.cumsum(ragged_sizes(own, PACK_RECORDS, PACK_TOKENS, PACK_TOKENS // 2, 0)), jnp.arange(PACK_TOKENS), side="right"))(jax.random.split(part_splits[2], N_DP)).reshape((N_DP, PACK_TOKENS)).astype(jnp.int32),
        "query_weight": centred(splits[3], (MODEL_WIDTH, MODEL_WIDTH), MODEL_WIDTH ** -0.5, 0.0546875, ((0, 8),)),
        "adapter_down_weight": centred(splits[4], (MODEL_WIDTH, ADAPTER_RANK), MODEL_WIDTH ** -0.5, 0.0546875, ((0, 8),)),
        "adapter_up_weight": centred(splits[5], (ADAPTER_RANK, MODEL_WIDTH), MODEL_WIDTH ** -0.5, 0.0546875, ((1, 8),)),
    }


ADAPTER_SCALE = 2.0

def spread_matrix(values, record_lookup, record_slots):
    onehot = (record_lookup[:, None] == record_slots[None, :]).astype(jnp.bfloat16)
    return (values[:, None, :] * onehot[:, :, None]).reshape(values.shape[0], record_slots.shape[0] * values.shape[1])

def squares(matrix, groups):
    return lax.optimization_barrier(jnp.sum(jnp.square(matrix.reshape(groups, -1)), axis=1))

def reference(tokens, cotangent, token_record_index, query_weight, adapter_down_weight, adapter_up_weight):
    record_slots = jnp.arange(PACK_RECORDS, dtype=jnp.int32)
    clipping_limit = ADAPTER_SCALE * math.sqrt(2.0 * MODEL_WIDTH * ADAPTER_RANK * PACK_TOKENS / PACK_RECORDS)
    query_outputs = []
    sum_a = jnp.zeros((ADAPTER_RANK, MODEL_WIDTH), jnp.float32)
    sum_b = jnp.zeros((ADAPTER_RANK, MODEL_WIDTH), jnp.float32)
    for pack_index in range(N_DP):
        token_inputs = tokens[pack_index]
        upstream_gradient = cotangent[pack_index]
        record_lookup = token_record_index[pack_index].astype(jnp.int32)
        down_projected = jnp.dot(token_inputs, adapter_down_weight, preferred_element_type=jnp.float32).astype(jnp.bfloat16)
        base_output = jnp.dot(token_inputs, query_weight, preferred_element_type=jnp.float32)
        adapted_output = jnp.dot(down_projected, adapter_up_weight, preferred_element_type=jnp.float32)
        query_outputs.append((base_output + ADAPTER_SCALE * adapted_output).astype(jnp.bfloat16))
        backward_term = jnp.dot(upstream_gradient, adapter_up_weight.T, preferred_element_type=jnp.float32).astype(jnp.bfloat16)
        down_gradient = ADAPTER_SCALE * jnp.dot(spread_matrix(backward_term, record_lookup, record_slots).T, token_inputs, preferred_element_type=jnp.float32)
        up_gradient = ADAPTER_SCALE * jnp.dot(spread_matrix(down_projected, record_lookup, record_slots).T, upstream_gradient, preferred_element_type=jnp.float32)
        norms = squares(down_gradient, PACK_RECORDS) + squares(up_gradient, PACK_RECORDS)
        factor = jnp.minimum(1.0, clipping_limit * lax.rsqrt(norms + 1e-06))
        sum_a = sum_a + lax.optimization_barrier(jnp.sum(down_gradient.reshape(PACK_RECORDS, ADAPTER_RANK, MODEL_WIDTH) * factor[:, None, None], axis=0))
        sum_b = sum_b + lax.optimization_barrier(jnp.sum(up_gradient.reshape(PACK_RECORDS, ADAPTER_RANK, MODEL_WIDTH) * factor[:, None, None], axis=0))
    scale = 1.0 / (N_DP * PACK_RECORDS)
    return (jnp.stack(query_outputs), sum_a * scale, sum_b * scale)
```

```python
import functools
import math

import jax
import jax.numpy as jnp
from jax import lax
from jax.experimental import pallas as pl
from jax.experimental.pallas import tpu as pltpu
from jax.sharding import PartitionSpec as P

PACK_RECORDS = 4
ADAPTER_SCALE = 2.0
W_SLOTS = 4
EARLY = 3


def kernel(
    n_tp, n_dp, clip, cw,
    tok_ref, cot_ref, idx_ref, wq_ref, ad_ref, au_ref,
    query_ref, ga_ref, gb_ref,
    wbuf, ysend, yrecv, acc, zsend, zrecv, small, norms, grad, pair,
    w_sem, ys_sem, yr_sem, zs_sem, zr_sem, ss_sem, sr_sem, ns_sem, nr_sem, ps_sem, pr_sem,
):
    f32, bf16 = jnp.float32, jnp.bfloat16
    tokens, depth = tok_ref.shape
    rank = au_ref.shape[0]
    cols = query_ref.shape[1]
    subs = cols // cw
    n_z = n_tp // 2
    items = n_z * subs
    me = lax.axis_index("tp")
    core = lax.axis_index("dp")
    my_z, my_y = me // 2, lax.rem(me, 2)
    other_y = 1 - my_y
    partner = my_z * 2 + other_y

    def dest_z(item):
        step = item // subs
        order = jnp.where(step == n_z - 1, 0, lax.rem(step + n_z // 2, n_z))
        order = jnp.where((step >= n_z // 2) & (step < n_z - 1), step - n_z // 2 + 1, order)
        return lax.rem(my_z + order, n_z)

    def w_copy(step):
        half = step // items
        item = lax.rem(step, items)
        y = jnp.where(half == 0, other_y, my_y)
        col = (dest_z(item) * 2 + y) * cols + lax.rem(item, subs) * cw
        slot = lax.rem(step, W_SLOTS)
        return pltpu.make_async_copy(
            wq_ref.at[:, pl.ds(pl.multiple_of(col, 128), cw)], wbuf.at[slot], w_sem.at[slot]
        )

    def product(step):
        w_copy(step).wait()
        return jnp.dot(tok_ref[...], wbuf[lax.rem(step, W_SLOTS)], preferred_element_type=f32)

    def prefetch(step):
        @pl.when(step + W_SLOTS < 2 * items)
        def _():
            w_copy(step + W_SLOTS).start()

    def y_copy(item):
        return pltpu.make_async_remote_copy(
            src_ref=ysend.at[item], dst_ref=yrecv.at[item],
            send_sem=ys_sem.at[item], recv_sem=yr_sem.at[item],
            device_id={"tp": partner}, device_id_type=pl.DeviceIdType.MESH,
        )

    def z_copy(item):
        sub = lax.rem(item, subs)
        return pltpu.make_async_remote_copy(
            src_ref=zsend.at[item], dst_ref=zrecv.at[my_z * subs + sub],
            send_sem=zs_sem.at[item], recv_sem=zr_sem.at[my_z * subs + sub],
            device_id={"tp": dest_z(item) * 2 + my_y}, device_id_type=pl.DeviceIdType.MESH,
        )

    def z_arrival(slot):
        return pltpu.make_async_remote_copy(
            src_ref=zrecv.at[slot], dst_ref=zrecv.at[slot],
            send_sem=zs_sem.at[0], recv_sem=zr_sem.at[slot],
            device_id={"tp": partner}, device_id_type=pl.DeviceIdType.MESH,
        )

    def share(buf, slot, peer, send, recv):
        return pltpu.make_async_remote_copy(
            src_ref=buf.at[slot], dst_ref=buf.at[slot],
            send_sem=send.at[peer], recv_sem=recv.at[slot],
            device_id={"tp": peer}, device_id_type=pl.DeviceIdType.MESH,
        )

    def over_peers(fn):
        def body(j, carry):
            fn(lax.rem(me + j, n_tp))
            return carry

        lax.fori_loop(1, n_tp, body, 0)

    for step in range(W_SLOTS):
        w_copy(step).start()

    barrier = pltpu.get_barrier_semaphore()
    over_peers(lambda peer: pl.semaphore_signal(
        barrier, inc=1, device_id={"tp": peer}, device_id_type=pl.DeviceIdType.MESH))
    for d in range(1, n_dp):
        pl.semaphore_signal(
            barrier, inc=1, device_id={"dp": lax.rem(core + d, n_dp)},
            device_id_type=pl.DeviceIdType.MESH)
    pl.semaphore_wait(barrier, n_tp + n_dp - 2)

    nt = (((1,), (1,)), ((), ()))
    small[me, pl.ds(0, rank), :] = lax.dot_general(
        ad_ref[...], tok_ref[...], nt, preferred_element_type=f32)
    small[me, pl.ds(rank, rank), :] = lax.dot_general(
        au_ref[...], cot_ref[...], nt, preferred_element_type=f32)
    over_peers(lambda peer: share(small, me, peer, ss_sem, sr_sem).start())

    def y_step(item, carry):
        ysend[item] = product(item).astype(bf16)
        y_copy(item).start()
        prefetch(item)
        return carry

    early = min(EARLY, items)
    lax.fori_loop(0, early, y_step, 0)

    over_peers(lambda peer: share(small, peer, peer, ss_sem, sr_sem).wait_recv())
    total = small[0]
    for j in range(1, n_tp):
        total = total + small[j]
    down = total[:rank].astype(bf16)
    back = total[rank:].astype(bf16)
    record = idx_ref[...]

    def spread(values):
        return jnp.concatenate(
            [jnp.where(record == r, values, jnp.zeros_like(values)) for r in range(PACK_RECORDS)],
            axis=0,
        )

    grad[0] = ADAPTER_SCALE * jnp.dot(spread(back), tok_ref[...], preferred_element_type=f32)
    grad[1] = ADAPTER_SCALE * jnp.dot(spread(down), cot_ref[...], preferred_element_type=f32)
    for r in range(PACK_RECORDS):
        rows = pl.ds(r * rank, rank)
        ga, gb = grad[0, rows, :], grad[1, rows, :]
        square = jnp.sum(jnp.sum(ga * ga + gb * gb, axis=0, keepdims=True), axis=1, keepdims=True)
        norms[me, pl.ds(r * 8, 8), :] = jnp.broadcast_to(square, (8, 128))
    over_peers(lambda peer: share(norms, me, peer, ns_sem, nr_sem).start())

    lax.fori_loop(early, items, y_step, 0)

    def own_step(item, carry):
        acc[item] = product(item + items)
        prefetch(item + items)
        return carry

    lax.fori_loop(0, items, own_step, 0)

    own0 = items - subs
    lanes = down.astype(f32).T.astype(bf16)
    for sub in range(subs):
        acc[own0 + sub] += ADAPTER_SCALE * jnp.dot(
            lanes, au_ref[:, pl.ds(sub * cw, cw)], preferred_element_type=f32)

    over_peers(lambda peer: share(norms, peer, peer, ns_sem, nr_sem).wait_recv())
    norm = norms[0]
    for j in range(1, n_tp):
        norm = norm + norms[j]
    factor = jnp.minimum(1.0, clip * lax.rsqrt(norm + 1e-06))
    for side in range(2):
        part = jnp.zeros((rank, cols), f32)
        for r in range(PACK_RECORDS):
            part = part + grad[side, pl.ds(r * rank, rank), :] * factor[r * 8:r * 8 + 1, 0:1]
        pair[core, pl.ds(side * rank, rank), :] = part

    def pair_copy(slot, other):
        return pltpu.make_async_remote_copy(
            src_ref=pair.at[slot], dst_ref=pair.at[slot],
            send_sem=ps_sem.at[other], recv_sem=pr_sem.at[slot],
            device_id={"dp": other}, device_id_type=pl.DeviceIdType.MESH,
        )

    for d in range(1, n_dp):
        pair_copy(core, lax.rem(core + d, n_dp)).start()

    def z_step(item, carry):
        y_copy(item).wait_recv()
        zsend[item] = (acc[item] + yrecv[item].astype(f32)).astype(bf16)
        z_copy(item).start()
        return carry

    lax.fori_loop(0, own0, z_step, 0)

    for d in range(1, n_dp):
        other = lax.rem(core + d, n_dp)
        pair_copy(other, other).wait_recv()
    both = pair[0]
    for d in range(1, n_dp):
        both = both + pair[d]
    scale = 1.0 / (n_dp * PACK_RECORDS)
    ga_ref[...] = both[:rank] * scale
    gb_ref[...] = both[rank:] * scale

    def own_sum(item, carry):
        y_copy(item).wait_recv()
        acc[item] += yrecv[item].astype(f32)
        return carry

    lax.fori_loop(own0, items, own_sum, 0)

    for sub in range(subs):
        def arrive(j, carry):
            slot = lax.rem(my_z + j, n_z) * subs + sub
            z_arrival(slot).wait_recv()
            acc[own0 + sub] += zrecv[slot].astype(f32)
            return carry

        lax.fori_loop(1, n_z, arrive, 0)
        query_ref[:, pl.ds(sub * cw, cw)] = acc[own0 + sub].astype(bf16)

    def y_done(item, carry):
        y_copy(item).wait_send()
        return carry

    lax.fori_loop(0, items, y_done, 0)

    def z_done(item, carry):
        z_copy(item).wait_send()
        return carry

    lax.fori_loop(0, own0, z_done, 0)
    over_peers(lambda peer: share(small, me, peer, ss_sem, sr_sem).wait_send())
    over_peers(lambda peer: share(norms, me, peer, ns_sem, nr_sem).wait_send())
    for d in range(1, n_dp):
        pair_copy(core, lax.rem(core + d, n_dp)).wait_send()


def local(n_tp, n_dp, tokens, cotangent, index, query_weight, down_weight, up_weight):
    f32, bf16 = jnp.float32, jnp.bfloat16
    rows, depth = tokens.shape[1:]
    rank, cols = up_weight.shape
    width = query_weight.shape[1]
    clip = ADAPTER_SCALE * math.sqrt(2.0 * width * rank * rows / PACK_RECORDS)
    cw = 512 if cols % 512 == 0 else cols
    subs = cols // cw
    n_z = n_tp // 2
    items = n_z * subs
    dma = pltpu.SemaphoreType.DMA
    vmem = pl.BlockSpec(memory_space=pltpu.VMEM)
    query, grad_a, grad_b = pl.pallas_call(
        functools.partial(kernel, n_tp, n_dp, clip, cw),
        out_shape=(
            jax.ShapeDtypeStruct((rows, cols), bf16),
            jax.ShapeDtypeStruct((rank, cols), f32),
            jax.ShapeDtypeStruct((rank, cols), f32),
        ),
        in_specs=[vmem, vmem, vmem, pl.BlockSpec(memory_space=pl.ANY), vmem, vmem],
        out_specs=(vmem, vmem, vmem),
        scratch_shapes=[
            pltpu.VMEM((W_SLOTS, depth, cw), bf16),
            pltpu.VMEM((items, rows, cw), bf16),
            pltpu.VMEM((items, rows, cw), bf16),
            pltpu.VMEM((items, rows, cw), f32),
            pltpu.VMEM((items - subs, rows, cw), bf16),
            pltpu.VMEM((items, rows, cw), bf16),
            pltpu.VMEM((n_tp, 2 * rank, rows), f32),
            pltpu.VMEM((n_tp, 8 * PACK_RECORDS, 128), f32),
            pltpu.VMEM((2, PACK_RECORDS * rank, cols), f32),
            pltpu.VMEM((n_dp, 2 * rank, cols), f32),
            dma((W_SLOTS,)),
            dma((items,)),
            dma((items,)),
            dma((items,)),
            dma((items,)),
            dma((n_tp,)),
            dma((n_tp,)),
            dma((n_tp,)),
            dma((n_tp,)),
            dma((n_dp,)),
            dma((n_dp,)),
        ],
        compiler_params=pltpu.CompilerParams(
            collective_id=0, has_side_effects=True, vmem_limit_bytes=60 * 1024 * 1024),
        cost_estimate=pl.CostEstimate(
            flops=2 * rows * depth * width, bytes_accessed=2 * depth * width, transcendentals=0),
    )(tokens[0], cotangent[0], index, query_weight, down_weight.T, up_weight)
    return query[None], grad_a, grad_b


def solution(mesh):
    placed = (
        P(("parts", "dp"), None, "tp"),
        P(("parts", "dp"), None, "tp"),
        P(("parts", "dp"), None),
        P("tp", None),
        P("tp", None),
        P(None, "tp"),
    )
    return jax.shard_map(
        functools.partial(local, mesh.shape["tp"], mesh.shape["dp"]),
        mesh=mesh,
        in_specs=placed,
        out_specs=(P(("parts", "dp"), None, "tp"), P("parts", "tp"), P("parts", "tp")),
        check_vma=False,
    )
```

```python
import functools
import math

import jax
import jax.numpy as jnp
from jax import lax
from jax.experimental import pallas as pl
from jax.experimental.pallas import tpu as pltpu
from jax.sharding import PartitionSpec as P

PACK_RECORDS = 4
ADAPTER_SCALE = 2.0
W_SLOTS = 4
EARLY = 3
AHEAD = 2
P_FIRST = 1


def kernel(
    n_tp, n_dp, clip, cw,
    tok_ref, cot_ref, idx_ref, wq_ref, ad_ref, au_ref,
    query_ref, ga_ref, gb_ref,
    wbuf, send1, recv1, acc, send2, recv2, send3, recv3, small, norms, grad, pair,
    w_sem, s1_sem, r1_sem, s2_sem, r2_sem, s3_sem, r3_sem, ss_sem, sr_sem, ns_sem, nr_sem, ps_sem, pr_sem,
):
    f32, bf16 = jnp.float32, jnp.bfloat16
    tokens, depth = tok_ref.shape
    rank = au_ref.shape[0]
    cols = query_ref.shape[1]
    subs = cols // cw
    n_h = n_tp // 4
    items = 2 * n_h * subs
    me = lax.axis_index("tp")
    core = lax.axis_index("dp")
    my_h, my_p, my_y = me // 4, lax.rem(me // 2, 2), lax.rem(me, 2)
    y_mate = me + 1 - 2 * my_y
    p_mate = me + 2 - 4 * my_p

    def dest_h(hi):
        return lax.rem(my_h + hi + 1, n_h)

    def at(hi, pi, s):
        return (hi * 2 + pi) * subs + s

    def w_copy(step):
        own = step // items
        item = lax.rem(step, items)
        s = lax.rem(item, subs)
        pi = lax.rem(item // subs, 2)
        hi = item // (2 * subs)
        p_first = s < P_FIRST
        y = jnp.where(jnp.where(p_first, pi, own) == 1, my_y, 1 - my_y)
        p = jnp.where(jnp.where(p_first, own, pi) == 1, my_p, 1 - my_p)
        col = (dest_h(hi) * 4 + p * 2 + y) * cols + s * cw
        slot = lax.rem(step, W_SLOTS)
        return pltpu.make_async_copy(
            wq_ref.at[:, pl.ds(pl.multiple_of(col, 128), cw)], wbuf.at[slot], w_sem.at[slot]
        )

    def product(step):
        w_copy(step).wait()
        return jnp.dot(tok_ref[...], wbuf[lax.rem(step, W_SLOTS)], preferred_element_type=f32)

    def prefetch(step):
        @pl.when(step + W_SLOTS < 2 * items)
        def _():
            w_copy(step + W_SLOTS).start()

    def first_copy(item):
        s = lax.rem(item, subs)
        return pltpu.make_async_remote_copy(
            src_ref=send1.at[item], dst_ref=recv1.at[item],
            send_sem=s1_sem.at[item], recv_sem=r1_sem.at[item],
            device_id={"tp": jnp.where(s < P_FIRST, p_mate, y_mate)},
            device_id_type=pl.DeviceIdType.MESH,
        )

    def second_copy(hi, s):
        i = hi * subs + s
        return pltpu.make_async_remote_copy(
            src_ref=send2.at[i], dst_ref=recv2.at[i],
            send_sem=s2_sem.at[i], recv_sem=r2_sem.at[i],
            device_id={"tp": jnp.where(s < P_FIRST, y_mate, p_mate)},
            device_id_type=pl.DeviceIdType.MESH,
        )

    def third_copy(hi, s):
        i = hi * subs + s
        return pltpu.make_async_remote_copy(
            src_ref=send3.at[i], dst_ref=recv3.at[my_h * subs + s],
            send_sem=s3_sem.at[i], recv_sem=r3_sem.at[my_h * subs + s],
            device_id={"tp": dest_h(hi) * 4 + my_p * 2 + my_y},
            device_id_type=pl.DeviceIdType.MESH,
        )

    def third_arrival(h, s):
        i = h * subs + s
        return pltpu.make_async_remote_copy(
            src_ref=recv3.at[i], dst_ref=recv3.at[i],
            send_sem=s3_sem.at[0], recv_sem=r3_sem.at[i],
            device_id={"tp": y_mate}, device_id_type=pl.DeviceIdType.MESH,
        )

    def share(buf, slot, peer, send, recv):
        return pltpu.make_async_remote_copy(
            src_ref=buf.at[slot], dst_ref=buf.at[slot],
            send_sem=send.at[peer], recv_sem=recv.at[slot],
            device_id={"tp": peer}, device_id_type=pl.DeviceIdType.MESH,
        )

    def over_peers(fn):
        def body(j, carry):
            fn(lax.rem(me + j, n_tp))
            return carry

        lax.fori_loop(1, n_tp, body, 0)

    for step in range(W_SLOTS):
        w_copy(step).start()

    barrier = pltpu.get_barrier_semaphore()
    over_peers(lambda peer: pl.semaphore_signal(
        barrier, inc=1, device_id={"tp": peer}, device_id_type=pl.DeviceIdType.MESH))
    for d in range(1, n_dp):
        pl.semaphore_signal(
            barrier, inc=1, device_id={"dp": lax.rem(core + d, n_dp)},
            device_id_type=pl.DeviceIdType.MESH)
    pl.semaphore_wait(barrier, n_tp + n_dp - 2)

    nt = (((1,), (1,)), ((), ()))
    small[me, pl.ds(0, rank), :] = lax.dot_general(
        ad_ref[...], tok_ref[...], nt, preferred_element_type=f32)
    small[me, pl.ds(rank, rank), :] = lax.dot_general(
        au_ref[...], cot_ref[...], nt, preferred_element_type=f32)
    over_peers(lambda peer: share(small, me, peer, ss_sem, sr_sem).start())

    def first_step(item, carry):
        send1[item] = product(item).astype(bf16)

        @pl.when((item < AHEAD * subs) | (lax.rem(item, subs) < P_FIRST))
        def _():
            first_copy(item).start()

        prefetch(item)
        return carry

    early = min(EARLY, items)
    lax.fori_loop(0, early, first_step, 0)

    over_peers(lambda peer: share(small, peer, peer, ss_sem, sr_sem).wait_recv())
    total = small[0]
    for j in range(1, n_tp):
        total = total + small[j]
    down = total[:rank].astype(bf16)
    back = total[rank:].astype(bf16)
    record = idx_ref[...]

    def spread(values):
        return jnp.concatenate(
            [jnp.where(record == r, values, jnp.zeros_like(values)) for r in range(PACK_RECORDS)],
            axis=0,
        )

    grad[0] = ADAPTER_SCALE * jnp.dot(spread(back), tok_ref[...], preferred_element_type=f32)
    grad[1] = ADAPTER_SCALE * jnp.dot(spread(down), cot_ref[...], preferred_element_type=f32)
    for r in range(PACK_RECORDS):
        rows = pl.ds(r * rank, rank)
        ga, gb = grad[0, rows, :], grad[1, rows, :]
        square = jnp.sum(jnp.sum(ga * ga + gb * gb, axis=0, keepdims=True), axis=1, keepdims=True)
        norms[me, pl.ds(r * 8, 8), :] = jnp.broadcast_to(square, (8, 128))
    over_peers(lambda peer: share(norms, me, peer, ns_sem, nr_sem).start())

    lax.fori_loop(early, items, first_step, 0)

    def own_step(item, carry):
        acc[item] = product(item + items)
        prefetch(item + items)
        return carry

    lax.fori_loop(0, items, own_step, 0)

    own0 = at(n_h - 1, 1, 0)
    lanes = down.astype(f32).T.astype(bf16)
    for sub in range(subs):
        acc[own0 + sub] += ADAPTER_SCALE * jnp.dot(
            lanes, au_ref[:, pl.ds(sub * cw, cw)], preferred_element_type=f32)

    over_peers(lambda peer: share(norms, peer, peer, ns_sem, nr_sem).wait_recv())
    norm = norms[0]
    for j in range(1, n_tp):
        norm = norm + norms[j]
    factor = jnp.minimum(1.0, clip * lax.rsqrt(norm + 1e-06))
    for side in range(2):
        part = jnp.zeros((rank, cols), f32)
        for r in range(PACK_RECORDS):
            part = part + grad[side, pl.ds(r * rank, rank), :] * factor[r * 8:r * 8 + 1, 0:1]
        pair[core, pl.ds(side * rank, rank), :] = part

    def pair_copy(slot, other):
        return pltpu.make_async_remote_copy(
            src_ref=pair.at[slot], dst_ref=pair.at[slot],
            send_sem=ps_sem.at[other], recv_sem=pr_sem.at[slot],
            device_id={"dp": other}, device_id_type=pl.DeviceIdType.MESH,
        )

    for d in range(1, n_dp):
        pair_copy(core, lax.rem(core + d, n_dp)).start()

    def add_first(hi, pi, s):
        item = at(hi, pi, s)
        first_copy(item).wait_recv()
        return acc[item] + recv1[item].astype(f32)

    def pass_second(hi, s):
        send2[hi * subs + s] = add_first(hi, 0, s).astype(bf16)
        second_copy(hi, s).start()

    def add_second(hi, s, value):
        second_copy(hi, s).wait_recv()
        return value + recv2[hi * subs + s].astype(f32)

    def pass_third(hi, s, value):
        send3[hi * subs + s] = value.astype(bf16)
        third_copy(hi, s).start()

    def more(hi, pi, s):
        nxt = at(hi, pi, s) + AHEAD * subs

        @pl.when(nxt < items)
        def _():
            first_copy(nxt).start()

    def p_first_step(hi, carry):
        for s in range(P_FIRST):
            pass_second(hi, s)
            acc[at(hi, 1, s)] = add_first(hi, 1, s)
        return carry

    lax.fori_loop(0, n_h, p_first_step, 0)

    def far_step(hi, carry):
        def other_place(s, c):
            pass_second(hi, s)
            more(hi, 0, s)
            return c

        def own_place(s, c):
            value = add_first(hi, 1, s)
            more(hi, 1, s)
            pass_third(hi, s, add_second(hi, s, value))
            return c

        lax.fori_loop(P_FIRST, subs, other_place, 0)
        lax.fori_loop(P_FIRST, subs, own_place, 0)
        for s in range(P_FIRST):
            pass_third(hi, s, add_second(hi, s, acc[at(hi, 1, s)]))
        return carry

    lax.fori_loop(0, n_h - 1, far_step, 0)

    for d in range(1, n_dp):
        other = lax.rem(core + d, n_dp)
        pair_copy(other, other).wait_recv()
    both = pair[0]
    for d in range(1, n_dp):
        both = both + pair[d]
    scale = 1.0 / (n_dp * PACK_RECORDS)
    ga_ref[...] = both[:rank] * scale
    gb_ref[...] = both[rank:] * scale

    last = n_h - 1

    def last_other(s, carry):
        pass_second(last, s)
        return carry

    lax.fori_loop(P_FIRST, subs, last_other, 0)

    for s in range(subs):
        value = acc[own0 + s] if s < P_FIRST else add_first(last, 1, s)
        acc[own0 + s] = add_second(last, s, value)

        def arrive(j, carry):
            h = lax.rem(my_h + j, n_h)
            third_arrival(h, s).wait_recv()
            acc[own0 + s] += recv3[h * subs + s].astype(f32)
            return carry

        lax.fori_loop(1, n_h, arrive, 0)
        query_ref[:, pl.ds(s * cw, cw)] = acc[own0 + s].astype(bf16)

    def first_done(item, carry):
        first_copy(item).wait_send()
        return carry

    lax.fori_loop(0, items, first_done, 0)

    def second_done(i, carry):
        second_copy(i // subs, lax.rem(i, subs)).wait_send()
        return carry

    lax.fori_loop(0, n_h * subs, second_done, 0)

    def third_done(i, carry):
        third_copy(i // subs, lax.rem(i, subs)).wait_send()
        return carry

    lax.fori_loop(0, last * subs, third_done, 0)
    over_peers(lambda peer: share(small, me, peer, ss_sem, sr_sem).wait_send())
    over_peers(lambda peer: share(norms, me, peer, ns_sem, nr_sem).wait_send())
    for d in range(1, n_dp):
        pair_copy(core, lax.rem(core + d, n_dp)).wait_send()


def local(n_tp, n_dp, tokens, cotangent, index, query_weight, down_weight, up_weight):
    f32, bf16 = jnp.float32, jnp.bfloat16
    rows, depth = tokens.shape[1:]
    rank, cols = up_weight.shape
    width = query_weight.shape[1]
    clip = ADAPTER_SCALE * math.sqrt(2.0 * width * rank * rows / PACK_RECORDS)
    subs = 4 if cols % 512 == 0 else 3
    cw = cols // subs
    n_h = n_tp // 4
    items = 2 * n_h * subs
    dma = pltpu.SemaphoreType.DMA
    vmem = pl.BlockSpec(memory_space=pltpu.VMEM)
    query, grad_a, grad_b = pl.pallas_call(
        functools.partial(kernel, n_tp, n_dp, clip, cw),
        out_shape=(
            jax.ShapeDtypeStruct((rows, cols), bf16),
            jax.ShapeDtypeStruct((rank, cols), f32),
            jax.ShapeDtypeStruct((rank, cols), f32),
        ),
        in_specs=[vmem, vmem, vmem, pl.BlockSpec(memory_space=pl.ANY), vmem, vmem],
        out_specs=(vmem, vmem, vmem),
        scratch_shapes=[
            pltpu.VMEM((W_SLOTS, depth, cw), bf16),
            pltpu.VMEM((items, rows, cw), bf16),
            pltpu.VMEM((items, rows, cw), bf16),
            pltpu.VMEM((items, rows, cw), f32),
            pltpu.VMEM((n_h * subs, rows, cw), bf16),
            pltpu.VMEM((n_h * subs, rows, cw), bf16),
            pltpu.VMEM(((n_h - 1) * subs, rows, cw), bf16),
            pltpu.VMEM((n_h * subs, rows, cw), bf16),
            pltpu.VMEM((n_tp, 2 * rank, rows), f32),
            pltpu.VMEM((n_tp, 8 * PACK_RECORDS, 128), f32),
            pltpu.VMEM((2, PACK_RECORDS * rank, cols), f32),
            pltpu.VMEM((n_dp, 2 * rank, cols), f32),
            dma((W_SLOTS,)),
            dma((items,)),
            dma((items,)),
            dma((n_h * subs,)),
            dma((n_h * subs,)),
            dma(((n_h - 1) * subs,)),
            dma((n_h * subs,)),
            dma((n_tp,)),
            dma((n_tp,)),
            dma((n_tp,)),
            dma((n_tp,)),
            dma((n_dp,)),
            dma((n_dp,)),
        ],
        compiler_params=pltpu.CompilerParams(
            collective_id=0, has_side_effects=True, vmem_limit_bytes=60 * 1024 * 1024),
        cost_estimate=pl.CostEstimate(
            flops=2 * rows * depth * width, bytes_accessed=2 * depth * width, transcendentals=0),
    )(tokens[0], cotangent[0], index, query_weight, down_weight.T, up_weight)
    return query[None], grad_a, grad_b


def solution(mesh):
    placed = (
        P(("parts", "dp"), None, "tp"),
        P(("parts", "dp"), None, "tp"),
        P(("parts", "dp"), None),
        P("tp", None),
        P("tp", None),
        P(None, "tp"),
    )
    return jax.shard_map(
        functools.partial(local, mesh.shape["tp"], mesh.shape["dp"]),
        mesh=mesh,
        in_specs=placed,
        out_specs=(P(("parts", "dp"), None, "tp"), P("parts", "tp"), P("parts", "tp")),
        check_vma=False,
    )
```

```python
import functools
import math

import jax
import jax.numpy as jnp
from jax import lax
from jax.experimental import pallas as pl
from jax.experimental.pallas import tpu as pltpu
from jax.sharding import PartitionSpec as P

PACK_RECORDS = 4
ADAPTER_SCALE = 2.0
W_SLOTS = 4
EARLY = 3
AHEAD = 2
P_FIRST = 1


def kernel(
    n_tp, n_dp, clip, cw,
    tok_ref, cot_ref, idx_ref, wq_ref, ad_ref, au_ref,
    query_ref, ga_ref, gb_ref,
    wbuf, send1, recv1, acc, send2, recv2, send3, recv3, small, norms, grad, pair,
    w_sem, s1_sem, r1_sem, s2_sem, r2_sem, s3_sem, r3_sem, ss_sem, sr_sem, ns_sem, nr_sem, ps_sem, pr_sem,
):
    f32, bf16 = jnp.float32, jnp.bfloat16
    tokens, depth = tok_ref.shape
    rank = au_ref.shape[0]
    cols = query_ref.shape[1]
    subs = cols // cw
    n_h = n_tp // 4
    group = 2 * subs
    items = n_h * group
    me = lax.axis_index("tp")
    core = lax.axis_index("dp")
    my_h, my_p, my_y = me // 4, lax.rem(me // 2, 2), lax.rem(me, 2)
    y_mate = me + 1 - 2 * my_y
    p_mate = me + 2 - 4 * my_p

    def dest_h(hi):
        return lax.rem(my_h + hi + 1, n_h)

    def at(hi, pi, s):
        return (hi * 2 + pi) * subs + s

    def w_copy(step):
        early, middle, late = step < group, step < items, step < 2 * items - group
        own = jnp.where(early | (jnp.logical_not(middle) & late), 0, 1)
        item = step - jnp.where(
            early, 0, jnp.where(middle, group, jnp.where(late, items - group, items)))
        s = lax.rem(item, subs)
        pi = lax.rem(item // subs, 2)
        hi = item // (2 * subs)
        p_first = s < P_FIRST
        y = jnp.where(jnp.where(p_first, pi, own) == 1, my_y, 1 - my_y)
        p = jnp.where(jnp.where(p_first, own, pi) == 1, my_p, 1 - my_p)
        col = (dest_h(hi) * 4 + p * 2 + y) * cols + s * cw
        slot = lax.rem(step, W_SLOTS)
        return pltpu.make_async_copy(
            wq_ref.at[:, pl.ds(pl.multiple_of(col, 128), cw)], wbuf.at[slot], w_sem.at[slot]
        )

    def product(step):
        w_copy(step).wait()
        return jnp.dot(tok_ref[...], wbuf[lax.rem(step, W_SLOTS)], preferred_element_type=f32)

    def prefetch(step):
        @pl.when(step + W_SLOTS < 2 * items)
        def _():
            w_copy(step + W_SLOTS).start()

    def first_copy(item):
        s = lax.rem(item, subs)
        return pltpu.make_async_remote_copy(
            src_ref=send1.at[item], dst_ref=recv1.at[item],
            send_sem=s1_sem.at[item], recv_sem=r1_sem.at[item],
            device_id={"tp": jnp.where(s < P_FIRST, p_mate, y_mate)},
            device_id_type=pl.DeviceIdType.MESH,
        )

    def second_copy(hi, s):
        i = hi * subs + s
        return pltpu.make_async_remote_copy(
            src_ref=send2.at[i], dst_ref=recv2.at[i],
            send_sem=s2_sem.at[i], recv_sem=r2_sem.at[i],
            device_id={"tp": jnp.where(s < P_FIRST, y_mate, p_mate)},
            device_id_type=pl.DeviceIdType.MESH,
        )

    def third_copy(hi, s):
        i = hi * subs + s
        return pltpu.make_async_remote_copy(
            src_ref=send3.at[i], dst_ref=recv3.at[my_h * subs + s],
            send_sem=s3_sem.at[i], recv_sem=r3_sem.at[my_h * subs + s],
            device_id={"tp": dest_h(hi) * 4 + my_p * 2 + my_y},
            device_id_type=pl.DeviceIdType.MESH,
        )

    def third_arrival(h, s):
        i = h * subs + s
        return pltpu.make_async_remote_copy(
            src_ref=recv3.at[i], dst_ref=recv3.at[i],
            send_sem=s3_sem.at[0], recv_sem=r3_sem.at[i],
            device_id={"tp": y_mate}, device_id_type=pl.DeviceIdType.MESH,
        )

    def share(buf, slot, peer, send, recv):
        return pltpu.make_async_remote_copy(
            src_ref=buf.at[slot], dst_ref=buf.at[slot],
            send_sem=send.at[peer], recv_sem=recv.at[slot],
            device_id={"tp": peer}, device_id_type=pl.DeviceIdType.MESH,
        )

    def over_peers(fn):
        def body(j, carry):
            fn(lax.rem(me + j, n_tp))
            return carry

        lax.fori_loop(1, n_tp, body, 0)

    for step in range(W_SLOTS):
        w_copy(step).start()

    barrier = pltpu.get_barrier_semaphore()
    over_peers(lambda peer: pl.semaphore_signal(
        barrier, inc=1, device_id={"tp": peer}, device_id_type=pl.DeviceIdType.MESH))
    for d in range(1, n_dp):
        pl.semaphore_signal(
            barrier, inc=1, device_id={"dp": lax.rem(core + d, n_dp)},
            device_id_type=pl.DeviceIdType.MESH)
    pl.semaphore_wait(barrier, n_tp + n_dp - 2)

    nt = (((1,), (1,)), ((), ()))
    small[me, pl.ds(0, rank), :] = lax.dot_general(
        ad_ref[...], tok_ref[...], nt, preferred_element_type=f32)
    small[me, pl.ds(rank, rank), :] = lax.dot_general(
        au_ref[...], cot_ref[...], nt, preferred_element_type=f32)
    over_peers(lambda peer: share(small, me, peer, ss_sem, sr_sem).start())

    def first_step(item, carry):
        step = jnp.where(item < group, item, item + items - group)
        send1[item] = product(step).astype(bf16)

        @pl.when((item < AHEAD * subs) | (lax.rem(item, subs) < P_FIRST))
        def _():
            first_copy(item).start()

        prefetch(step)
        return carry

    def own_step(item, carry):
        step = jnp.where(item < items - group, item + group, item + items)
        acc[item] = product(step)
        prefetch(step)
        return carry

    lax.fori_loop(0, EARLY, first_step, 0)

    over_peers(lambda peer: share(small, peer, peer, ss_sem, sr_sem).wait_recv())
    total = small[0]
    for j in range(1, n_tp):
        total = total + small[j]
    down = total[:rank].astype(bf16)
    back = total[rank:].astype(bf16)
    record = idx_ref[...]

    def spread(values):
        return jnp.concatenate(
            [jnp.where(record == r, values, jnp.zeros_like(values)) for r in range(PACK_RECORDS)],
            axis=0,
        )

    grad[0] = ADAPTER_SCALE * jnp.dot(spread(back), tok_ref[...], preferred_element_type=f32)
    grad[1] = ADAPTER_SCALE * jnp.dot(spread(down), cot_ref[...], preferred_element_type=f32)
    for r in range(PACK_RECORDS):
        rows = pl.ds(r * rank, rank)
        ga, gb = grad[0, rows, :], grad[1, rows, :]
        square = jnp.sum(jnp.sum(ga * ga + gb * gb, axis=0, keepdims=True), axis=1, keepdims=True)
        norms[me, pl.ds(r * 8, 8), :] = jnp.broadcast_to(square, (8, 128))
    over_peers(lambda peer: share(norms, me, peer, ns_sem, nr_sem).start())

    lax.fori_loop(EARLY, group, first_step, 0)
    lax.fori_loop(0, items - group, own_step, 0)
    lax.fori_loop(group, items, first_step, 0)

    def add_first(hi, pi, s):
        item = at(hi, pi, s)
        first_copy(item).wait_recv()
        return acc[item] + recv1[item].astype(f32)

    def pass_second(hi, s):
        send2[hi * subs + s] = add_first(hi, 0, s).astype(bf16)
        second_copy(hi, s).start()

    def add_second(hi, s, value):
        second_copy(hi, s).wait_recv()
        return value + recv2[hi * subs + s].astype(f32)

    def pass_third(hi, s, value):
        send3[hi * subs + s] = value.astype(bf16)
        third_copy(hi, s).start()

    def more(hi, pi, s):
        nxt = at(hi, pi, s) + AHEAD * subs

        @pl.when(nxt < items)
        def _():
            first_copy(nxt).start()

    def p_first_step(hi, carry):
        for s in range(P_FIRST):
            pass_second(hi, s)
            acc[at(hi, 1, s)] = add_first(hi, 1, s)
        return carry

    def other_place(hi):
        def body(s, carry):
            pass_second(hi, s)
            more(hi, 0, s)
            return carry

        lax.fori_loop(P_FIRST, subs, body, 0)

    last = n_h - 1
    lax.fori_loop(0, last, p_first_step, 0)
    other_place(0)

    lax.fori_loop(items - group, items, own_step, 0)
    p_first_step(last, 0)

    own0 = at(n_h - 1, 1, 0)
    lanes = down.astype(f32).T.astype(bf16)
    for sub in range(subs):
        acc[own0 + sub] += ADAPTER_SCALE * jnp.dot(
            lanes, au_ref[:, pl.ds(sub * cw, cw)], preferred_element_type=f32)

    over_peers(lambda peer: share(norms, peer, peer, ns_sem, nr_sem).wait_recv())
    norm = norms[0]
    for j in range(1, n_tp):
        norm = norm + norms[j]
    factor = jnp.minimum(1.0, clip * lax.rsqrt(norm + 1e-06))
    for side in range(2):
        part = jnp.zeros((rank, cols), f32)
        for r in range(PACK_RECORDS):
            part = part + grad[side, pl.ds(r * rank, rank), :] * factor[r * 8:r * 8 + 1, 0:1]
        pair[core, pl.ds(side * rank, rank), :] = part

    def pair_copy(slot, other):
        return pltpu.make_async_remote_copy(
            src_ref=pair.at[slot], dst_ref=pair.at[slot],
            send_sem=ps_sem.at[other], recv_sem=pr_sem.at[slot],
            device_id={"dp": other}, device_id_type=pl.DeviceIdType.MESH,
        )

    for d in range(1, n_dp):
        pair_copy(core, lax.rem(core + d, n_dp)).start()

    def far_step(hi, carry):
        def own_place(s, c):
            value = add_first(hi, 1, s)
            more(hi, 1, s)
            pass_third(hi, s, add_second(hi, s, value))
            return c

        lax.fori_loop(P_FIRST, subs, own_place, 0)
        for s in range(P_FIRST):
            pass_third(hi, s, add_second(hi, s, acc[at(hi, 1, s)]))
        other_place(hi + 1)
        return carry

    lax.fori_loop(0, last, far_step, 0)

    for d in range(1, n_dp):
        other = lax.rem(core + d, n_dp)
        pair_copy(other, other).wait_recv()
    both = pair[0]
    for d in range(1, n_dp):
        both = both + pair[d]
    scale = 1.0 / (n_dp * PACK_RECORDS)
    ga_ref[...] = both[:rank] * scale
    gb_ref[...] = both[rank:] * scale

    for s in range(subs):
        value = acc[own0 + s] if s < P_FIRST else add_first(last, 1, s)
        acc[own0 + s] = add_second(last, s, value)

        def arrive(j, carry):
            h = lax.rem(my_h + j, n_h)
            third_arrival(h, s).wait_recv()
            acc[own0 + s] += recv3[h * subs + s].astype(f32)
            return carry

        lax.fori_loop(1, n_h, arrive, 0)
        query_ref[:, pl.ds(s * cw, cw)] = acc[own0 + s].astype(bf16)

    def first_done(item, carry):
        first_copy(item).wait_send()
        return carry

    lax.fori_loop(0, items, first_done, 0)

    def second_done(i, carry):
        second_copy(i // subs, lax.rem(i, subs)).wait_send()
        return carry

    lax.fori_loop(0, n_h * subs, second_done, 0)

    def third_done(i, carry):
        third_copy(i // subs, lax.rem(i, subs)).wait_send()
        return carry

    lax.fori_loop(0, last * subs, third_done, 0)
    over_peers(lambda peer: share(small, me, peer, ss_sem, sr_sem).wait_send())
    over_peers(lambda peer: share(norms, me, peer, ns_sem, nr_sem).wait_send())
    for d in range(1, n_dp):
        pair_copy(core, lax.rem(core + d, n_dp)).wait_send()


def local(n_tp, n_dp, tokens, cotangent, index, query_weight, down_weight, up_weight):
    f32, bf16 = jnp.float32, jnp.bfloat16
    rows, depth = tokens.shape[1:]
    rank, cols = up_weight.shape
    width = query_weight.shape[1]
    clip = ADAPTER_SCALE * math.sqrt(2.0 * width * rank * rows / PACK_RECORDS)
    subs = 4 if cols % 512 == 0 else 3
    cw = cols // subs
    n_h = n_tp // 4
    items = 2 * n_h * subs
    dma = pltpu.SemaphoreType.DMA
    vmem = pl.BlockSpec(memory_space=pltpu.VMEM)
    query, grad_a, grad_b = pl.pallas_call(
        functools.partial(kernel, n_tp, n_dp, clip, cw),
        out_shape=(
            jax.ShapeDtypeStruct((rows, cols), bf16),
            jax.ShapeDtypeStruct((rank, cols), f32),
            jax.ShapeDtypeStruct((rank, cols), f32),
        ),
        in_specs=[vmem, vmem, vmem, pl.BlockSpec(memory_space=pl.ANY), vmem, vmem],
        out_specs=(vmem, vmem, vmem),
        scratch_shapes=[
            pltpu.VMEM((W_SLOTS, depth, cw), bf16),
            pltpu.VMEM((items, rows, cw), bf16),
            pltpu.VMEM((items, rows, cw), bf16),
            pltpu.VMEM((items, rows, cw), f32),
            pltpu.VMEM((n_h * subs, rows, cw), bf16),
            pltpu.VMEM((n_h * subs, rows, cw), bf16),
            pltpu.VMEM(((n_h - 1) * subs, rows, cw), bf16),
            pltpu.VMEM((n_h * subs, rows, cw), bf16),
            pltpu.VMEM((n_tp, 2 * rank, rows), f32),
            pltpu.VMEM((n_tp, 8 * PACK_RECORDS, 128), f32),
            pltpu.VMEM((2, PACK_RECORDS * rank, cols), f32),
            pltpu.VMEM((n_dp, 2 * rank, cols), f32),
            dma((W_SLOTS,)),
            dma((items,)),
            dma((items,)),
            dma((n_h * subs,)),
            dma((n_h * subs,)),
            dma(((n_h - 1) * subs,)),
            dma((n_h * subs,)),
            dma((n_tp,)),
            dma((n_tp,)),
            dma((n_tp,)),
            dma((n_tp,)),
            dma((n_dp,)),
            dma((n_dp,)),
        ],
        compiler_params=pltpu.CompilerParams(
            collective_id=0, has_side_effects=True, vmem_limit_bytes=60 * 1024 * 1024),
        cost_estimate=pl.CostEstimate(
            flops=2 * rows * depth * width, bytes_accessed=2 * depth * width, transcendentals=0),
    )(tokens[0], cotangent[0], index, query_weight, down_weight.T, up_weight)
    return query[None], grad_a, grad_b


def solution(mesh):
    placed = (
        P(("parts", "dp"), None, "tp"),
        P(("parts", "dp"), None, "tp"),
        P(("parts", "dp"), None),
        P("tp", None),
        P("tp", None),
        P(None, "tp"),
    )
    return jax.shard_map(
        functools.partial(local, mesh.shape["tp"], mesh.shape["dp"]),
        mesh=mesh,
        in_specs=placed,
        out_specs=(P(("parts", "dp"), None, "tp"), P("parts", "tp"), P("parts", "tp")),
        check_vma=False,
    )
```
